32 devices in a mesh: sec: 2 (over core), lat: 4 (over z), lon: 4 (over y, x).
Axes of the slice: x: 2, y: 2, z: 4, core: 2. Of those that a mesh axis runs over, the one named last changes fastest.
Arguments:
- adjoint_end: float32 [3, 16, 256, 1024], P(None, None, 'lat', ('sec', 'lon')), may hold values from -6 to 6
- east_flow: bfloat16 [16, 256, 1024], P(None, 'lat', ('sec', 'lon')), may hold values from -0.079589844 to 0.079589844
- east_diff: bfloat16 [16, 256, 1024], P(None, 'lat', ('sec', 'lon')), may hold values from 0.039794922 to 0.119628906
- north_flow: bfloat16 [16, 256, 1024], P(None, 'lat', ('sec', 'lon')), may hold values from -0.079589844 to 0.079589844
- north_diff: bfloat16 [16, 256, 1024], P(None, 'lat', ('sec', 'lon')), may hold values from 0.039794922 to 0.119628906
- vert_diff: bfloat16 [15, 256, 1024], P(None, 'lat', ('sec', 'lon')), may hold values from 0.019897461 to 0.1796875
- ocean_mask: int32 [256, 1024], P('lat', ('sec', 'lon')), may hold values 0 or 1
- reaction: float32 [3, 3], replicated, may hold values from -0.05 to 0.05
- solubility: float32 [3, 256, 1024], P(None, 'lat', ('sec', 'lon')), may hold values from 0.1 to 1
- route_tile: int32 [8, 256, 1], P(None, 'lat'), may hold values from 0 to 7; in each aligned block of 64 rows (0 to 63, 64 to 127, ..., all dimensions but the last counted through in order) at most 16 rows name the same one
- route_block: int32 [8, 256], P(None, 'lat'), may hold values from 0 to 31
- xgrid_weights: bfloat16 [256, 1024, 128], P('lat', ('sec', 'lon')), may hold values from -0.5 to 0.5
- deposition: bfloat16 [32, 128, 1024], P(None, 'lat', ('sec', 'lon')), may hold values from 0.19921875 to 2
Outputs:
- adjoint_start: float32 [3, 16, 256, 1024], P(None, None, 'lat', ('sec', 'lon'))
- flux_adjoint: float32 [128, 1024], P('lat', ('sec', 'lon'))
- ash_adjoint: float32 [32, 128, 1024], P(None, 'lat', ('sec', 'lon'))
The draws below stay inside these ranges and needn't reach their ends.
Inputs may be any that keep to these rules, and one draw needn't show every extreme that they name: `route_tile`: among the 64 rows of one device (aligned blocks of 64 rows, in the order of the first two dimensions) no tile is named more than 16 times, a bound that some block reaches.
All inputs are finite; a program needn't handle non-finite values. No bound on the sum of `ocean_mask` on one device may be relied on, other than what follows from the above.
Results may differ from the reference program's by a relative error of at most 0.0029.
Values may be sent and summed in bfloat16 or wider, within the bound.
A program may use at most 128 MiB of HBM per device.

```python
import math
import jax
import jax.numpy as jnp
import numpy as np
from jax import lax

CY = 64
BLK = 128
LEV = 16
NTR = 3
ALEV = 32
NSTEP = 16
NT = 8
NY = 256
NX = 1024
ABLK = 32
NA = 128
CAP = 16


def set_ends(values, key, low, top_value):
    extent = values.shape
    index_at = [jax.random.randint(jax.random.fold_in(key, axis), (), 0, extent[axis]) for axis in range(len(extent))]
    values = values.at[tuple(index_at)].set(low)
    longest = extent.index(max(extent))
    index_at[longest] = (index_at[longest] + 1) % extent[longest]
    return values.at[tuple(index_at)].set(top_value)


def block_scale(stream_key, extent, cuts, smallest, top_value):
    def one(dim, parts):
        draws = jax.random.uniform(jax.random.fold_in(jax.random.fold_in(stream_key, 6), dim), (parts,), jnp.float32, smallest / len(cuts), top_value / len(cuts))
        return jnp.repeat(jnp.exp(draws), extent[dim] // parts).reshape((-1,) + (1,) * (len(extent) - dim - 1))

    gain = one(*cuts[0])
    for cut in cuts[1:]:
        gain = gain * one(*cut)
    return gain


def assign_block(rng, own, number, rows, amount, top, bound, skew):
    ranking = jax.random.permutation(rng, amount)
    heavy_load, usual = load_shares(amount, rows * top, bound, skew, True), load_shares(amount, rows * top, bound, skew, False)
    places = jnp.arange(amount)

    def named(lengths, rotation):
        used = int((lengths > 0).sum())
        fixed = max(1, used // 4)
        passed = fixed + (places - fixed + rotation * (used - fixed)) % max(1, amount - fixed)
        return jnp.zeros((amount,), jnp.int32).at[ranking[jnp.where(places < fixed, places, passed)]].set(jnp.asarray(lengths, jnp.int32))

    lengths = jnp.where(number % 4 == 0, named(heavy_load, number // 4), named(usual, number - number // 4 - 1))
    mixed = jax.random.permutation(jax.random.fold_in(own, 3), amount)
    source_of, taker = mixed[0:amount // 2 * 2:2], mixed[1:amount // 2 * 2:2]
    room = jnp.minimum(lengths[source_of] - 1, bound - lengths[taker]) // 2
    room = jnp.where((source_of == ranking[0]) | (taker == ranking[0]) | (lengths[taker] == 0), 0, jnp.maximum(room, 0))
    passed = jax.random.randint(jax.random.fold_in(own, 4), (amount // 2,), 0, 1 << 20) % (room + 1)
    lengths = lengths.at[source_of].add(-passed).at[taker].add(passed)
    members = jnp.searchsorted(jnp.cumsum(lengths), jnp.arange(rows * top), side="right").astype(jnp.int32)
    table = members.reshape(top, rows).T
    table = table[jax.random.permutation(jax.random.fold_in(own, 1), rows)]
    rotation = jax.random.randint(jax.random.fold_in(own, 2), (rows, 1), 0, top)
    return jnp.take_along_axis(table, (jnp.arange(top)[None, :] + rotation) % top, axis=1)


def load_shares(number_of, total, bound, lean, full):
    portions = [(1 << 20) // math.isqrt(grade ** lean) + 1 for grade in range(1, number_of + 1)]
    largest = bound if full else min(bound, max(-(-total // number_of), total * portions[0] // sum(portions)))
    least = 1 if total - largest >= number_of - 1 else 0
    given, surplus = [largest] + [least] * (number_of - 1), total - largest - least * (number_of - 1)
    while surplus > 0:
        free = [i for i in range(1, number_of) if given[i] < largest] or [i for i in range(1, number_of) if given[i] < bound]
        mass, remaining = sum([portions[i] for i in free]), surplus
        for i in free:
            more = min(bound - given[i], max(1, remaining * portions[i] // mass), surplus)
            given[i] = given[i] + more
            surplus = surplus - more
    return np.array(given)


def centred(stream_key, dims, scale, most, split=(), held_as=jnp.bfloat16):
    result = jax.random.normal(stream_key, dims, jnp.float32) * scale
    if len(split) > 0:
        result = block_scale(stream_key, dims, split, -0.22, 0.18) * result
    return jnp.clip(result, min=-most, max=most).astype(held_as)


def setup_inputs(seed: int = 0) -> dict:
    streams_of = jax.random.split(jax.random.key(seed), 14)
    adjoint_end = centred(streams_of[0], (NTR, LEV, NY, NX), 1.0, 6.0, ((2, 4), (3, 8)), jnp.float32)
    east_flow = jnp.clip(jax.random.uniform(streams_of[1], (LEV, NY, NX), jnp.float32, -0.079589844, 0.079589844) * block_scale(streams_of[1], (LEV, NY, NX), ((1, 4), (2, 8)), -0.4, 0.0), -0.079589844, 0.079589844).astype(jnp.bfloat16)
    east_diff = jnp.clip(jnp.exp(math.log(0.119628906) - 1.1006552 * jax.random.uniform(streams_of[2], (LEV, NY, NX), jnp.float32) ** block_scale(streams_of[2], (LEV, NY, NX), ((1, 4), (2, 8)), -0.2, 0.2)), 0.039794922, 0.119628906).astype(jnp.bfloat16)
    north_flow = jnp.clip(jax.random.uniform(streams_of[3], (LEV, NY, NX), jnp.float32, -0.079589844, 0.079589844) * block_scale(streams_of[3], (LEV, NY, NX), ((1, 4), (2, 8)), -0.4, 0.0), -0.079589844, 0.079589844).astype(jnp.bfloat16)
    north_diff = jnp.clip(jnp.exp(math.log(0.119628906) - 1.1006552 * jax.random.uniform(streams_of[4], (LEV, NY, NX), jnp.float32) ** block_scale(streams_of[4], (LEV, NY, NX), ((1, 4), (2, 8)), -0.2, 0.2)), 0.039794922, 0.119628906).astype(jnp.bfloat16)
    vert_diff = jnp.clip(jnp.exp(math.log(0.1796875) - 2.200627 * jax.random.uniform(streams_of[5], (LEV - 1, NY, NX), jnp.float32) ** block_scale(streams_of[5], (LEV - 1, NY, NX), ((1, 4), (2, 8)), -0.2, 0.2)), 0.019897461, 0.1796875).astype(jnp.bfloat16)
    ocean_mask = set_ends((jax.random.randint(streams_of[6], (NY, NX), 0, 8) < 7).astype(jnp.int32), jax.random.fold_in(streams_of[6], 1), 0, 1)
    reaction = jnp.clip(jax.random.uniform(streams_of[7], (NTR, NTR), jnp.float32, -0.05, 0.05), -0.05, 0.05)
    solubility = jnp.clip(jnp.exp(math.log(1.0) - 2.3025851 * jax.random.uniform(streams_of[8], (NTR, NY, NX), jnp.float32) ** block_scale(streams_of[8], (NTR, NY, NX), ((1, 4), (2, 8)), -0.2, 0.2)), 0.1, 1.0)
    route_tile_keys = jax.random.split(jax.random.fold_in(streams_of[9], 1), NT * NY // CY)
    route_tile_turns = jax.random.permutation(jax.random.fold_in(streams_of[9], 3), NT * NY // CY)
    route_tile = jax.vmap(lambda own, number: assign_block(jax.random.fold_in(streams_of[9], 2), own, number, CY, NT, 1, CAP, 2))(route_tile_keys, route_tile_turns).reshape((NT, NY, 1))
    route_block = set_ends(jax.random.randint(streams_of[10], (NT, NY), 0, ABLK), jax.random.fold_in(streams_of[10], 1), 0, ABLK - 1).astype(jnp.int32)
    xgrid_weights = centred(streams_of[11], (NY, NX, BLK), BLK ** -0.5, 0.5, ((0, 4), (1, 8)))
    deposition = jnp.clip(jnp.exp(math.log(2.0) - 2.306499 * jax.random.uniform(streams_of[12], (ALEV, NA, NX), jnp.float32) ** block_scale(streams_of[12], (ALEV, NA, NX), ((1, 4), (2, 8)), -0.2, 0.2)), 0.19921875, 2.0).astype(jnp.bfloat16)
    return {"adjoint_end": adjoint_end, "east_flow": east_flow, "east_diff": east_diff, "north_flow": north_flow, "north_diff": north_diff, "vert_diff": vert_diff, "ocean_mask": ocean_mask, "reaction": reaction, "solubility": solubility, "route_tile": route_tile, "route_block": route_block, "xgrid_weights": xgrid_weights, "deposition": deposition}


def face_pair(flow, diffusion, open_face):
    speed = flow.astype(jnp.float32)
    spread = diffusion.astype(jnp.float32)
    return (0.5 * speed + spread) * open_face, (0.5 * speed - spread) * open_face


def reference(adjoint_end, east_flow, east_diff, north_flow, north_diff, vert_diff, ocean_mask, reaction, solubility, route_tile, route_block, xgrid_weights, deposition):
    ocean_plane = ocean_mask.astype(jnp.float32)
    east_open = ocean_plane * jnp.roll(ocean_plane, -1, axis=1)
    north_open = ocean_plane * jnp.concatenate([ocean_plane[1:], jnp.zeros_like(ocean_plane[:1])], 0)
    east_fwd, east_back = face_pair(east_flow, east_diff, east_open)
    north_fwd, north_back = face_pair(north_flow, north_diff, north_open)
    west_back = jnp.roll(east_back, 1, axis=2)
    south_back = jnp.concatenate([jnp.zeros_like(north_back[:, :1]), north_back[:, :-1]], 1)
    vertical = vert_diff.astype(jnp.float32)
    tracers = adjoint_end.shape[0]

    def advance(adjoint):
        east_step = jnp.roll(adjoint, -1, axis=3) - adjoint
        west_step = adjoint - jnp.roll(adjoint, 1, axis=3)
        upper = jnp.concatenate([adjoint[:, :, 1:], jnp.zeros_like(adjoint[:, :, :1])], 2)
        lower = jnp.concatenate([jnp.zeros_like(adjoint[:, :, :1]), adjoint[:, :, :-1]], 2)
        change = (east_fwd * east_step + west_back * west_step
                  + north_fwd * (upper - adjoint) + south_back * (adjoint - lower))
        vert_flux = vertical * (adjoint[:, 1:] - adjoint[:, :-1])
        boundary = jnp.zeros_like(adjoint[:, :1])
        vert_change = jnp.concatenate([vert_flux, boundary], 1) - jnp.concatenate([boundary, vert_flux], 1)
        coupled = jnp.stack([sum(reaction[source, tracer] * adjoint[source] for source in range(tracers)) for tracer in range(tracers)])
        return ocean_plane * (adjoint + change + vert_change + coupled)

    def loop_step(counter, carry):
        adjoint, surface_sum = carry
        surface_sum = surface_sum + adjoint[:, 0]
        return advance(adjoint), surface_sum

    start_sum = jnp.zeros_like(adjoint_end[:, 0])
    adjoint_start, surface_sum = lax.fori_loop(0, NSTEP, loop_step, (adjoint_end, start_sum))
    tracer_sum = sum(solubility[tracer] * surface_sum[tracer] for tracer in range(tracers))
    flux_ocean = (ocean_plane * (tracer_sum * (1.0 / NSTEP))).astype(jnp.bfloat16)
    flux_rows = flux_ocean.reshape(NY, NT, BLK)
    weight_rows = xgrid_weights.reshape(NY, NT, BLK, BLK)

    def row_blocks(pieces):
        flux_one, weight_one = pieces
        return jnp.einsum('sb,sba->sa', flux_one.astype(jnp.float32), weight_one.astype(jnp.float32))

    blocks = lax.map(row_blocks, (flux_rows, weight_rows))
    band_of_row = jnp.arange(NY, dtype=jnp.int32) // CY
    target_rows = (band_of_row[None, :] * ABLK + route_block).astype(jnp.int32)
    target_tiles = route_tile[:, :, 0].astype(jnp.int32)
    gathered = jnp.zeros((NA, NT, BLK), jnp.float32).at[target_rows, target_tiles].add(jnp.transpose(blocks, (1, 0, 2)))
    flux_adjoint = gathered.reshape(NA, NT * BLK)
    ash_adjoint = deposition.astype(jnp.float32) * flux_adjoint[None]
    return adjoint_start, flux_adjoint, ash_adjoint
```

```python
import functools

import jax
import jax.numpy as jnp
from jax import lax
from jax.experimental import pallas as pl
from jax.experimental.pallas import tpu as pltpu
from jax.sharding import PartitionSpec as P

NSTEP = 16
F32 = jnp.float32
MESH = pl.DeviceIdType.MESH
CHUNKS = 2
SUB = 8
LANES = 128


def ocean_kernel(
    shape,
    reaction,
    adjoint_end,
    east_flow,
    east_diff,
    north_flow,
    north_diff,
    vert_diff,
    ocean_mask,
    solubility,
    start_out,
    flux_out,
    state,
    c_east,
    c_west,
    c_north,
    c_south,
    c_zero,
    c_vert,
    ocean,
    total,
    raw,
    x_send,
    x_recv,
    y_send,
    y_recv,
    cx_send,
    cx_recv,
    cy_send,
    cy_recv,
    send_sem,
    recv_sem,
    coef_send_sem,
    coef_recv_sem,
):
    sections, bands, tiles = shape
    tracers, levels = adjoint_end.shape[:2]
    per_chunk = levels // CHUNKS
    pairs = per_chunk // 2
    sec, lat, lon = lax.axis_index("sec"), lax.axis_index("lat"), lax.axis_index("lon")
    ring = sections * tiles
    place = sec * tiles + lon
    east = lax.rem(place + 1, ring)
    west = lax.rem(place + ring - 1, ring)
    to_east = (lax.div(east, tiles), lat, lax.rem(east, tiles))
    to_west = (lax.div(west, tiles), lat, lax.rem(west, tiles))
    to_north = (sec, lax.min(lat + 1, bands - 1), lon)
    to_south = (sec, lax.max(lat - 1, 0), lon)
    has_north, has_south = lat < bands - 1, lat > 0

    lane = lax.broadcasted_iota(jnp.int32, (SUB, LANES), 1)
    sub = lax.broadcasted_iota(jnp.int32, (SUB, LANES), 0)
    first_lane, last_lane = lane == 0, lane == LANES - 1
    first_sub, last_sub = sub == 0, sub == SUB - 1
    even = lax.rem(lane, 2) == 0
    pair_of = lax.div(lane, 2)

    def pack(packed, value, j):
        moved = pltpu.roll(value, 2 * j + 1, 1)
        return moved if packed is None else jnp.where(pair_of == j, moved, packed)

    def merge(from_west, from_east):
        return jnp.where(even, pltpu.roll(from_east, LANES - 1, 1), pltpu.roll(from_west, 1, 1))

    def edge(merged, j):
        return pltpu.roll(merged, LANES - 2 * j - 1, 1)

    def northward(values, i, row):
        if i < SUB - 1:
            return values[i + 1]
        return jnp.where(last_sub, row, pltpu.roll(values[0], SUB - 1, 0))

    def southward(values, i, row):
        if i > 0:
            return values[i - 1]
        return jnp.where(first_sub, row, pltpu.roll(values[SUB - 1], 1, 0))

    def spread(row):
        return jnp.broadcast_to(row, (SUB, LANES))

    def coef_copies():
        out = []
        for d, (src, dst, dev) in enumerate(
            (
                (cx_send, cx_recv.at[0], to_east),
                (cx_send, cx_recv.at[1], to_west),
                (cy_send.at[0], cy_recv.at[0], to_north),
                (cy_send.at[1], cy_recv.at[1], to_south),
            )
        ):
            out.append(
                pltpu.make_async_remote_copy(
                    src_ref=src,
                    dst_ref=dst,
                    send_sem=coef_send_sem.at[d],
                    recv_sem=coef_recv_sem.at[d],
                    device_id=dev,
                    device_id_type=MESH,
                )
            )
        return out

    def copies(slot, g):
        out = []
        for d, (src, dst, dev) in enumerate(
            (
                (x_send.at[slot, g], x_recv.at[0, slot, g], to_east),
                (x_send.at[slot, g], x_recv.at[1, slot, g], to_west),
                (y_send.at[0, slot, g], y_recv.at[0, slot, g], to_north),
                (y_send.at[1, slot, g], y_recv.at[1, slot, g], to_south),
            )
        ):
            out.append(
                pltpu.make_async_remote_copy(
                    src_ref=src,
                    dst_ref=dst,
                    send_sem=send_sem.at[slot, g, d],
                    recv_sem=recv_sem.at[slot, g, d],
                    device_id=dev,
                    device_id_type=MESH,
                )
            )
        return out

    def start(c):
        c[0].start()
        c[1].start()
        pl.when(has_north)(c[2].start)
        pl.when(has_south)(c[3].start)

    def wait_send(c):
        c[0].wait_send()
        c[1].wait_send()
        pl.when(has_north)(c[2].wait_send)
        pl.when(has_south)(c[3].wait_send)

    def wait_recv(c):
        c[0].wait_recv()
        c[1].wait_recv()
        pl.when(has_south)(c[2].wait_recv)
        pl.when(has_north)(c[3].wait_recv)

    y_recv[...] = jnp.zeros_like(y_recv)
    cy_recv[...] = jnp.zeros_like(cy_recv)

    barrier = pltpu.get_barrier_semaphore()
    for dev in (to_east, to_west):
        pl.semaphore_signal(barrier, inc=1, device_id=dev, device_id_type=MESH)

    @pl.when(has_north)
    def _():
        pl.semaphore_signal(barrier, inc=1, device_id=to_north, device_id_type=MESH)

    @pl.when(has_south)
    def _():
        pl.semaphore_signal(barrier, inc=1, device_id=to_south, device_id_type=MESH)

    peers = 2 + has_north.astype(jnp.int32) + has_south.astype(jnp.int32)
    pl.semaphore_wait(barrier, peers)

    for i in range(SUB):
        ocean[i] = ocean_mask[pl.ds(i, SUB, stride=SUB), :].astype(F32)

    @pl.loop(0, levels)
    def _(l):
        flow, diff = east_flow[l].astype(F32), east_diff[l].astype(F32)
        raw[0] = 0.5 * flow + diff
        raw[1] = 0.5 * flow - diff
        flow, diff = north_flow[l].astype(F32), north_diff[l].astype(F32)
        raw[2] = 0.5 * flow + diff
        raw[3] = 0.5 * flow - diff
        packed = None
        for i in range(SUB):
            rows = pl.ds(i, SUB, stride=SUB)
            here = ocean[i]
            c_east[l, i] = raw[0, rows, :] * here
            back = raw[1, rows, :] * here
            c_west[l, i] = back
            packed = pack(packed, jnp.where(first_lane, here, back), i)
            c_north[l, i] = raw[2, rows, :] * here
            back = raw[3, rows, :] * here
            c_south[l, i] = back
            if i == SUB - 1:
                cy_send[0, pl.ds(l, 1), :] = back[SUB - 1 :, :]
            if i == 0:
                cy_send[1, pl.ds(l, 1), :] = here[:1, :]
        cx_send[l] = packed

    start(coef_copies())

    zero_plane = jnp.zeros((SUB, SUB, LANES), F32)
    for slot in range(2):
        for t in range(tracers):
            state[slot, t, 0] = zero_plane
            state[slot, t, levels + 1] = zero_plane
    c_vert[0] = zero_plane
    c_vert[levels] = zero_plane
    total[...] = jnp.zeros_like(total)

    def hand_over(slot, g, lp, dl, t, values, packed):
        row = lp * 2 + dl
        for i in range(SUB):
            packed = pack(packed, values[i], dl * tracers * SUB + t * SUB + i)
        y_send[0, slot, g, t, pl.ds(row, 1), :] = values[SUB - 1][SUB - 1 :, :]
        y_send[1, slot, g, t, pl.ds(row, 1), :] = values[0][:1, :]
        return packed

    for g in range(CHUNKS):

        @pl.loop(0, pairs)
        def _(lp):
            packed = None
            for dl in range(2):
                l = g * per_chunk + lp * 2 + dl
                for t in range(tracers):
                    values = []
                    for i in range(SUB):
                        cell = adjoint_end[t, l, pl.ds(i, SUB, stride=SUB), :] * ocean[i]
                        state[0, t, l + 1, i] = cell
                        values.append(cell)
                    packed = hand_over(0, g, lp, dl, t, values, packed)
            x_send[0, g, lp] = packed

        start(copies(0, g))

    @pl.loop(0, levels - 1)
    def _(l):
        raw[0] = vert_diff[l].astype(F32)
        for i in range(SUB):
            c_vert[l + 1, i] = raw[0, pl.ds(i, SUB, stride=SUB), :]

    wait_recv(coef_copies())

    @pl.loop(0, levels)
    def _(l):
        merged = merge(cx_recv[0, l], cx_recv[1, l])
        below = spread(cy_recv[0, pl.ds(l, 1), :])
        above = spread(cy_recv[1, pl.ds(l, 1), :])
        masks = [ocean[i] for i in range(SUB)]
        backs = [c_south[l, i] for i in range(SUB)]
        for i in range(SUB):
            here = masks[i]
            side = edge(merged, i)
            east_fwd = c_east[l, i] * jnp.where(last_lane, side, pltpu.roll(here, LANES - 1, 1))
            west_back = jnp.where(first_lane, side, pltpu.roll(c_west[l, i], 1, 1)) * here
            north_fwd = c_north[l, i] * northward(masks, i, above)
            south_back = southward(backs, i, below) * here
            c_east[l, i] = east_fwd
            c_west[l, i] = -west_back
            c_north[l, i] = north_fwd
            c_south[l, i] = -south_back
            c_zero[l, i] = (
                1.0
                - east_fwd
                + west_back
                - north_fwd
                + south_back
                - c_vert[l, i]
                - c_vert[l + 1, i]
            )

    wait_send(coef_copies())

    rate = [[reaction[s, t] for t in range(tracers)] for s in range(tracers)]

    @pl.loop(0, NSTEP)
    def _(k):
        now = lax.rem(k, 2)
        new = 1 - now
        for t in range(tracers):
            total[t] += state[now, t, 1]
        for g in range(CHUNKS):
            wait_recv(copies(now, g))

            @pl.when(k >= 1)
            def _():
                wait_send(copies(new, g))

            @pl.loop(0, pairs)
            def _(lp):
                merged = merge(x_recv[0, now, g, lp], x_recv[1, now, g, lp])
                packed = None
                for dl in range(2):
                    row = lp * 2 + dl
                    l = g * per_chunk + row
                    cells = [
                        [state[now, t, l + 1, i] for i in range(SUB)] for t in range(tracers)
                    ]
                    below = [
                        spread(y_recv[0, now, g, t, pl.ds(row, 1), :]) for t in range(tracers)
                    ]
                    above = [
                        spread(y_recv[1, now, g, t, pl.ds(row, 1), :]) for t in range(tracers)
                    ]
                    results = [[] for t in range(tracers)]
                    for i in range(SUB):
                        zero, vert_up, vert_down = c_zero[l, i], c_vert[l + 1, i], c_vert[l, i]
                        ce, cw, cn, cs = c_east[l, i], c_west[l, i], c_north[l, i], c_south[l, i]
                        for t in range(tracers):
                            a = cells[t][i]
                            side = edge(merged, dl * tracers * SUB + t * SUB + i)
                            value = (zero + rate[t][t]) * a
                            for s in range(tracers):
                                if s != t:
                                    value += rate[s][t] * cells[s][i]
                            value += vert_up * state[now, t, l + 2, i]
                            value += vert_down * state[now, t, l, i]
                            value += cn * northward(cells[t], i, above[t])
                            value += cs * southward(cells[t], i, below[t])
                            value += ce * jnp.where(last_lane, side, pltpu.roll(a, LANES - 1, 1))
                            value += cw * jnp.where(first_lane, side, pltpu.roll(a, 1, 1))
                            state[new, t, l + 1, i] = value
                            results[t].append(value)
                    for t in range(tracers):
                        packed = hand_over(new, g, lp, dl, t, results[t], packed)
                x_send[new, g, lp] = packed

            @pl.when(k < NSTEP - 1)
            def _():
                start(copies(new, g))

    for g in range(CHUNKS):
        wait_send(copies((NSTEP - 1) % 2, g))

    for i in range(SUB):
        rows = pl.ds(i, SUB, stride=SUB)
        acc = solubility[0, rows, :] * total[0, i]
        for t in range(1, tracers):
            acc += solubility[t, rows, :] * total[t, i]
        flux_out[rows, :] = ocean[i] * (acc * (1.0 / NSTEP))

    @pl.loop(0, levels)
    def _(l):
        for t in range(tracers):
            for i in range(SUB):
                start_out[t, l, pl.ds(i, SUB, stride=SUB), :] = state[NSTEP % 2, t, l + 1, i]


def run_ocean(shape, args, reaction):
    adjoint_end = args[0]
    tracers, levels, rows, cols = adjoint_end.shape
    per_chunk = levels // CHUNKS
    pairs = per_chunk // 2
    tile = (SUB, LANES)
    vmem = pl.BlockSpec(memory_space=pltpu.VMEM)
    coef = pltpu.VMEM((levels, SUB) + tile, F32)
    return pl.pallas_call(
        functools.partial(ocean_kernel, shape),
        out_shape=(
            jax.ShapeDtypeStruct(adjoint_end.shape, F32),
            jax.ShapeDtypeStruct((rows, cols), F32),
        ),
        in_specs=[pl.BlockSpec(memory_space=pltpu.SMEM)] + [vmem] * len(args),
        out_specs=(vmem, vmem),
        scratch_shapes=[
            pltpu.VMEM((2, tracers, levels + 2, SUB) + tile, F32),
            coef,
            coef,
            coef,
            coef,
            coef,
            pltpu.VMEM((levels + 1, SUB) + tile, F32),
            pltpu.VMEM((SUB,) + tile, F32),
            pltpu.VMEM((tracers, SUB) + tile, F32),
            pltpu.VMEM((4, rows, cols), F32),
            pltpu.VMEM((2, CHUNKS, pairs) + tile, F32),
            pltpu.VMEM((2, 2, CHUNKS, pairs) + tile, F32),
            pltpu.VMEM((2, 2, CHUNKS, tracers, per_chunk, cols), F32),
            pltpu.VMEM((2, 2, CHUNKS, tracers, per_chunk, cols), F32),
            pltpu.VMEM((levels,) + tile, F32),
            pltpu.VMEM((2, levels) + tile, F32),
            pltpu.VMEM((2, levels, cols), F32),
            pltpu.VMEM((2, levels, cols), F32),
            pltpu.SemaphoreType.DMA((2, CHUNKS, 4)),
            pltpu.SemaphoreType.DMA((2, CHUNKS, 4)),
            pltpu.SemaphoreType.DMA((4,)),
            pltpu.SemaphoreType.DMA((4,)),
        ],
        compiler_params=pltpu.CompilerParams(
            collective_id=0, has_side_effects=True, vmem_limit_bytes=48 * 1024 * 1024
        ),
    )(reaction, *args)


def exclusive_rank(hot, axis):
    count = hot.shape[axis]
    before = (jnp.arange(count)[:, None] < jnp.arange(count)[None, :]).astype(F32)
    return jnp.moveaxis(jnp.tensordot(hot, before, axes=((axis,), (0,))), -1, axis)


def deliver(blocks, route_tile, route_block, atm_rows):
    senders = lax.axis_size(("sec", "lon"))
    own_index = lax.axis_index(("sec", "lon"))
    block_count = blocks.shape[0]
    cell_count = blocks.shape[1]
    capacity = max(2, 2 * block_count // senders)
    dest_tiles = route_tile[:, :, 0]
    peer_ids = jnp.arange(senders, dtype=jnp.int32)
    slot_ids = jnp.arange(capacity, dtype=jnp.int32).astype(F32)
    own_tiles = lax.dynamic_index_in_dim(dest_tiles, own_index, 0, keepdims=False)
    dest_hot = (own_tiles[:, None] == peer_ids[None, :]).astype(F32)
    order_rank = exclusive_rank(dest_hot, 0)
    slot_index = jnp.sum(order_rank * dest_hot, axis=1)
    slot_hot = (slot_index[:, None] == slot_ids[None, :]).astype(F32)
    selector = (dest_hot[:, :, None] * slot_hot[:, None, :]).reshape(
        block_count, senders * capacity
    )
    outgoing = jnp.dot(selector.T, blocks, precision=lax.Precision.HIGHEST).reshape(
        senders, capacity, cell_count
    )
    incoming = lax.all_to_all(outgoing, ("sec", "lon"), split_axis=0, concat_axis=0, tiled=True)
    arrived = (dest_tiles == own_index).astype(F32)
    arrival_rank = exclusive_rank(arrived, 1)
    slot_take = arrived[:, :, None] * (arrival_rank[:, :, None] == slot_ids[None, None, :]).astype(
        F32
    )
    block_hot = (
        route_block[:, :, None] == jnp.arange(atm_rows, dtype=jnp.int32)[None, None, :]
    ).astype(F32)
    placing = jnp.einsum("syc,sya->asc", slot_take, block_hot, precision=lax.Precision.HIGHEST)
    placing = placing.reshape(atm_rows, senders * capacity)
    return jnp.dot(
        placing, incoming.reshape(senders * capacity, cell_count), precision=lax.Precision.HIGHEST
    )


def per_device(
    shape,
    adjoint_end,
    east_flow,
    east_diff,
    north_flow,
    north_diff,
    vert_diff,
    ocean_mask,
    reaction,
    solubility,
    route_tile,
    route_block,
    xgrid_weights,
    deposition,
):
    adjoint_start, flux = run_ocean(
        shape,
        (
            adjoint_end,
            east_flow,
            east_diff,
            north_flow,
            north_diff,
            vert_diff,
            ocean_mask,
            solubility,
        ),
        reaction,
    )
    blocks = jnp.einsum(
        "bo,boa->ba", flux.astype(jnp.bfloat16), xgrid_weights, preferred_element_type=F32
    )
    flux_adjoint = deliver(blocks, route_tile, route_block, deposition.shape[1])
    ash_adjoint = deposition.astype(F32) * flux_adjoint[None]
    return (adjoint_start, flux_adjoint, ash_adjoint)


def solution(mesh):
    shape = (mesh.shape["sec"], mesh.shape["lat"], mesh.shape["lon"])
    field = P(None, "lat", ("sec", "lon"))
    in_specs = (
        P(None, None, "lat", ("sec", "lon")),
        field,
        field,
        field,
        field,
        field,
        P("lat", ("sec", "lon")),
        P(),
        field,
        P(None, "lat", None),
        P(None, "lat"),
        P("lat", ("sec", "lon"), None),
        field,
    )
    out_specs = (
        P(None, None, "lat", ("sec", "lon")),
        P("lat", ("sec", "lon")),
        field,
    )
    return jax.shard_map(
        functools.partial(per_device, shape),
        mesh=mesh,
        in_specs=in_specs,
        out_specs=out_specs,
        check_vma=False,
    )
```

```python
import functools

import jax
import jax.numpy as jnp
from jax import lax
from jax.experimental import pallas as pl
from jax.experimental.pallas import tpu as pltpu
from jax.sharding import PartitionSpec as P

NSTEP = 16
F32 = jnp.float32
MESH = pl.DeviceIdType.MESH
CHUNKS = 4
SUB = 8
LANES = 128


def ocean_kernel(
    shape,
    reaction,
    adjoint_end_in,
    east_flow_in,
    east_diff_in,
    north_flow_in,
    north_diff_in,
    vert_diff_in,
    ocean_mask_in,
    solubility_in,
    start_out,
    flux_out,
    adjoint_end,
    east_flow,
    east_diff,
    north_flow,
    north_diff,
    vert_diff,
    ocean_mask,
    solubility,
    state_even,
    state_odd,
    c_east,
    c_west,
    c_north,
    c_south,
    c_zero,
    c_vert,
    ocean,
    total,
    raw,
    x_send,
    x_recv,
    y_send,
    y_recv,
    cx_send,
    cx_recv,
    cy_send,
    cy_recv,
    send_sem,
    recv_sem,
    coef_send_sem,
    coef_recv_sem,
    load_sem,
):
    sections, bands, tiles = shape
    tracers, levels = adjoint_end.shape[:2]
    per_chunk = levels // CHUNKS
    pairs = per_chunk // 2
    sec, lat, lon = lax.axis_index("sec"), lax.axis_index("lat"), lax.axis_index("lon")
    ring = sections * tiles
    place = sec * tiles + lon
    east = lax.rem(place + 1, ring)
    west = lax.rem(place + ring - 1, ring)
    to_east = (lax.div(east, tiles), lat, lax.rem(east, tiles))
    to_west = (lax.div(west, tiles), lat, lax.rem(west, tiles))
    to_north = (sec, lax.min(lat + 1, bands - 1), lon)
    to_south = (sec, lax.max(lat - 1, 0), lon)
    has_north, has_south = lat < bands - 1, lat > 0

    lane = lax.broadcasted_iota(jnp.int32, (SUB, LANES), 1)
    sub = lax.broadcasted_iota(jnp.int32, (SUB, LANES), 0)
    first_lane, last_lane = lane == 0, lane == LANES - 1
    first_sub, last_sub = sub == 0, sub == SUB - 1
    even = lax.rem(lane, 2) == 0
    pair_of = lax.div(lane, 2)

    def pack(packed, value, j):
        moved = pltpu.roll(value, 2 * j + 1, 1)
        return moved if packed is None else jnp.where(pair_of == j, moved, packed)

    def merge(from_west, from_east):
        return jnp.where(even, pltpu.roll(from_east, LANES - 1, 1), pltpu.roll(from_west, 1, 1))

    def edge(merged, j):
        return pltpu.roll(merged, LANES - 2 * j - 1, 1)

    def northward(values, i, row):
        if i < SUB - 1:
            return values[i + 1]
        return jnp.where(last_sub, row, pltpu.roll(values[0], SUB - 1, 0))

    def southward(values, i, row):
        if i > 0:
            return values[i - 1]
        return jnp.where(first_sub, row, pltpu.roll(values[SUB - 1], 1, 0))

    def spread(row):
        return jnp.broadcast_to(row, (SUB, LANES))

    def coef_copies():
        out = []
        for d, (src, dst, dev) in enumerate(
            (
                (cx_send, cx_recv.at[0], to_east),
                (cx_send, cx_recv.at[1], to_west),
                (cy_send.at[0], cy_recv.at[0], to_north),
                (cy_send.at[1], cy_recv.at[1], to_south),
            )
        ):
            out.append(
                pltpu.make_async_remote_copy(
                    src_ref=src,
                    dst_ref=dst,
                    send_sem=coef_send_sem.at[d],
                    recv_sem=coef_recv_sem.at[d],
                    device_id=dev,
                    device_id_type=MESH,
                )
            )
        return out

    def copies(slot, g):
        out = []
        for d, (src, dst, dev) in enumerate(
            (
                (x_send.at[slot, g], x_recv.at[0, slot, g], to_east),
                (x_send.at[slot, g], x_recv.at[1, slot, g], to_west),
                (y_send.at[0, slot, g], y_recv.at[0, slot, g], to_north),
                (y_send.at[1, slot, g], y_recv.at[1, slot, g], to_south),
            )
        ):
            out.append(
                pltpu.make_async_remote_copy(
                    src_ref=src,
                    dst_ref=dst,
                    send_sem=send_sem.at[slot, g, d],
                    recv_sem=recv_sem.at[slot, g, d],
                    device_id=dev,
                    device_id_type=MESH,
                )
            )
        return out

    def start(c):
        c[0].start()
        c[1].start()
        pl.when(has_north)(c[2].start)
        pl.when(has_south)(c[3].start)

    def wait_send(c):
        c[0].wait_send()
        c[1].wait_send()
        pl.when(has_north)(c[2].wait_send)
        pl.when(has_south)(c[3].wait_send)

    def wait_recv(c):
        c[0].wait_recv()
        c[1].wait_recv()
        pl.when(has_south)(c[2].wait_recv)
        pl.when(has_north)(c[3].wait_recv)

    loads = {}
    for n, (src, dst) in enumerate(
        (
            (ocean_mask_in, ocean_mask),
            (east_flow_in, east_flow),
            (east_diff_in, east_diff),
            (north_flow_in, north_flow),
            (north_diff_in, north_diff),
            (adjoint_end_in, adjoint_end),
            (vert_diff_in, vert_diff),
            (solubility_in, solubility),
        )
    ):
        loads[n] = pltpu.make_async_copy(src, dst, load_sem.at[n])
        loads[n].start()

    y_recv[...] = jnp.zeros_like(y_recv)
    cy_recv[...] = jnp.zeros_like(cy_recv)

    barrier = pltpu.get_barrier_semaphore()
    for dev in (to_east, to_west):
        pl.semaphore_signal(barrier, inc=1, device_id=dev, device_id_type=MESH)

    @pl.when(has_north)
    def _():
        pl.semaphore_signal(barrier, inc=1, device_id=to_north, device_id_type=MESH)

    @pl.when(has_south)
    def _():
        pl.semaphore_signal(barrier, inc=1, device_id=to_south, device_id_type=MESH)

    peers = 2 + has_north.astype(jnp.int32) + has_south.astype(jnp.int32)
    pl.semaphore_wait(barrier, peers)

    for n in range(5):
        loads[n].wait()
    for i in range(SUB):
        ocean[i] = ocean_mask[pl.ds(i, SUB, stride=SUB), :].astype(F32)

    @pl.loop(0, levels)
    def _(l):
        flow, diff = east_flow[l].astype(F32), east_diff[l].astype(F32)
        raw[0] = 0.5 * flow + diff
        raw[1] = 0.5 * flow - diff
        flow, diff = north_flow[l].astype(F32), north_diff[l].astype(F32)
        raw[2] = 0.5 * flow + diff
        raw[3] = 0.5 * flow - diff
        packed = None
        for i in range(SUB):
            rows = pl.ds(i, SUB, stride=SUB)
            here = ocean[i]
            c_east[l, i] = raw[0, rows, :] * here
            back = raw[1, rows, :] * here
            c_west[l, i] = back
            packed = pack(packed, jnp.where(first_lane, here, back), i)
            c_north[l, i] = raw[2, rows, :] * here
            back = raw[3, rows, :] * here
            c_south[l, i] = back
            if i == SUB - 1:
                cy_send[0, pl.ds(l, 1), :] = back[SUB - 1 :, :]
            if i == 0:
                cy_send[1, pl.ds(l, 1), :] = here[:1, :]
        cx_send[l] = packed

    start(coef_copies())

    zero_plane = jnp.zeros((SUB, SUB, LANES), F32)
    for state in (state_even, state_odd):
        for t in range(tracers):
            state[t, 0] = zero_plane
            state[t, levels + 1] = zero_plane
    c_vert[0] = zero_plane
    c_vert[levels] = zero_plane
    total[...] = jnp.zeros_like(total)

    def hand_over(slot, g, lp, dl, t, values, packed):
        row = lp * 2 + dl
        for i in range(SUB):
            packed = pack(packed, values[i], dl * tracers * SUB + t * SUB + i)
        y_send[0, slot, g, t, pl.ds(row, 1), :] = values[SUB - 1][SUB - 1 :, :]
        y_send[1, slot, g, t, pl.ds(row, 1), :] = values[0][:1, :]
        return packed

    loads[5].wait()
    for g in range(CHUNKS):

        @pl.loop(0, pairs)
        def _(lp):
            packed = None
            for dl in range(2):
                l = g * per_chunk + lp * 2 + dl
                for t in range(tracers):
                    values = []
                    for i in range(SUB):
                        cell = adjoint_end[t, l, pl.ds(i, SUB, stride=SUB), :] * ocean[i]
                        state_even[t, l + 1, i] = cell
                        values.append(cell)
                    packed = hand_over(0, g, lp, dl, t, values, packed)
            x_send[0, g, lp] = packed

        start(copies(0, g))

    loads[6].wait()

    @pl.loop(0, levels - 1)
    def _(l):
        raw[0] = vert_diff[l].astype(F32)
        for i in range(SUB):
            c_vert[l + 1, i] = raw[0, pl.ds(i, SUB, stride=SUB), :]

    wait_recv(coef_copies())

    @pl.loop(0, levels)
    def _(l):
        merged = merge(cx_recv[0, l], cx_recv[1, l])
        below = spread(cy_recv[0, pl.ds(l, 1), :])
        above = spread(cy_recv[1, pl.ds(l, 1), :])
        masks = [ocean[i] for i in range(SUB)]
        backs = [c_south[l, i] for i in range(SUB)]
        for i in range(SUB):
            here = masks[i]
            side = edge(merged, i)
            east_fwd = c_east[l, i] * jnp.where(last_lane, side, pltpu.roll(here, LANES - 1, 1))
            west_back = jnp.where(first_lane, side, pltpu.roll(c_west[l, i], 1, 1)) * here
            north_fwd = c_north[l, i] * northward(masks, i, above)
            south_back = southward(backs, i, below) * here
            c_east[l, i] = east_fwd
            c_west[l, i] = -west_back
            c_north[l, i] = north_fwd
            c_south[l, i] = -south_back
            c_zero[l, i] = (
                1.0
                - east_fwd
                + west_back
                - north_fwd
                + south_back
                - c_vert[l, i]
                - c_vert[l + 1, i]
            )

    wait_send(coef_copies())

    rate = [[reaction[s, t] for t in range(tracers)] for s in range(tracers)]

    def step(now, old, fresh, must_wait, must_send):
        new = 1 - now
        for t in range(tracers):
            total[t] += old[t, 1]
        for g in range(CHUNKS):
            wait_recv(copies(now, g))

            @pl.when(must_wait)
            def _():
                wait_send(copies(new, g))

            @pl.loop(0, pairs)
            def _(lp):
                merged = merge(x_recv[0, now, g, lp], x_recv[1, now, g, lp])
                packed = None
                for dl in range(2):
                    row = lp * 2 + dl
                    l = g * per_chunk + row
                    cells = [[old[t, l + 1, i] for i in range(SUB)] for t in range(tracers)]
                    below = [
                        spread(y_recv[0, now, g, t, pl.ds(row, 1), :]) for t in range(tracers)
                    ]
                    above = [
                        spread(y_recv[1, now, g, t, pl.ds(row, 1), :]) for t in range(tracers)
                    ]
                    for i in range(SUB):
                        zero, vert_up, vert_down = c_zero[l, i], c_vert[l + 1, i], c_vert[l, i]
                        ce, cw, cn, cs = c_east[l, i], c_west[l, i], c_north[l, i], c_south[l, i]
                        for t in range(tracers):
                            a = cells[t][i]
                            j = dl * tracers * SUB + t * SUB + i
                            side = edge(merged, j)
                            own = (zero + rate[t][t]) * a
                            for s in range(tracers):
                                if s != t:
                                    own += rate[s][t] * cells[s][i]
                            vert = vert_up * old[t, l + 2, i] + vert_down * old[t, l, i]
                            meridian = cn * northward(cells[t], i, above[t])
                            meridian += cs * southward(cells[t], i, below[t])
                            zonal = ce * jnp.where(last_lane, side, pltpu.roll(a, LANES - 1, 1))
                            zonal += cw * jnp.where(first_lane, side, pltpu.roll(a, 1, 1))
                            value = (own + vert) + (meridian + zonal)
                            fresh[t, l + 1, i] = value
                            packed = pack(packed, value, j)
                            if i == SUB - 1:
                                y_send[0, new, g, t, pl.ds(row, 1), :] = value[SUB - 1 :, :]
                            if i == 0:
                                y_send[1, new, g, t, pl.ds(row, 1), :] = value[:1, :]
                x_send[new, g, lp] = packed

            @pl.when(must_send)
            def _():
                start(copies(new, g))

    @pl.loop(0, NSTEP // 2)
    def _(k):
        step(0, state_even, state_odd, k >= 1, k >= 0)
        step(1, state_odd, state_even, k >= 0, k < NSTEP // 2 - 1)

    for g in range(CHUNKS):
        wait_send(copies((NSTEP - 1) % 2, g))

    loads[7].wait()
    for i in range(SUB):
        rows = pl.ds(i, SUB, stride=SUB)
        acc = solubility[0, rows, :] * total[0, i]
        for t in range(1, tracers):
            acc += solubility[t, rows, :] * total[t, i]
        flux_out[rows, :] = ocean[i] * (acc * (1.0 / NSTEP))

    @pl.loop(0, levels)
    def _(l):
        for t in range(tracers):
            for i in range(SUB):
                start_out[t, l, pl.ds(i, SUB, stride=SUB), :] = state_even[t, l + 1, i]


def run_ocean(shape, args, reaction):
    adjoint_end = args[0]
    tracers, levels, rows, cols = adjoint_end.shape
    per_chunk = levels // CHUNKS
    pairs = per_chunk // 2
    tile = (SUB, LANES)
    vmem = pl.BlockSpec(memory_space=pltpu.VMEM)
    coef = pltpu.VMEM((levels, SUB) + tile, F32)
    return pl.pallas_call(
        functools.partial(ocean_kernel, shape),
        out_shape=(
            jax.ShapeDtypeStruct(adjoint_end.shape, F32),
            jax.ShapeDtypeStruct((rows, cols), F32),
        ),
        in_specs=[pl.BlockSpec(memory_space=pltpu.SMEM)] + [pl.BlockSpec(memory_space=pl.ANY)] * len(args),
        out_specs=(vmem, vmem),
        scratch_shapes=[
            *[pltpu.VMEM(arg.shape, arg.dtype) for arg in args],
            pltpu.VMEM((tracers, levels + 2, SUB) + tile, F32),
            pltpu.VMEM((tracers, levels + 2, SUB) + tile, F32),
            coef,
            coef,
            coef,
            coef,
            coef,
            pltpu.VMEM((levels + 1, SUB) + tile, F32),
            pltpu.VMEM((SUB,) + tile, F32),
            pltpu.VMEM((tracers, SUB) + tile, F32),
            pltpu.VMEM((4, rows, cols), F32),
            pltpu.VMEM((2, CHUNKS, pairs) + tile, F32),
            pltpu.VMEM((2, 2, CHUNKS, pairs) + tile, F32),
            pltpu.VMEM((2, 2, CHUNKS, tracers, per_chunk, cols), F32),
            pltpu.VMEM((2, 2, CHUNKS, tracers, per_chunk, cols), F32),
            pltpu.VMEM((levels,) + tile, F32),
            pltpu.VMEM((2, levels) + tile, F32),
            pltpu.VMEM((2, levels, cols), F32),
            pltpu.VMEM((2, levels, cols), F32),
            pltpu.SemaphoreType.DMA((2, CHUNKS, 4)),
            pltpu.SemaphoreType.DMA((2, CHUNKS, 4)),
            pltpu.SemaphoreType.DMA((4,)),
            pltpu.SemaphoreType.DMA((4,)),
            pltpu.SemaphoreType.DMA((len(args),)),
        ],
        compiler_params=pltpu.CompilerParams(
            collective_id=0, has_side_effects=True, vmem_limit_bytes=48 * 1024 * 1024
        ),
    )(reaction, *args)


def exclusive_rank(hot, axis):
    count = hot.shape[axis]
    before = (jnp.arange(count)[:, None] < jnp.arange(count)[None, :]).astype(F32)
    return jnp.moveaxis(jnp.tensordot(hot, before, axes=((axis,), (0,))), -1, axis)


def deliver(blocks, route_tile, route_block, atm_rows):
    senders = lax.axis_size(("sec", "lon"))
    own_index = lax.axis_index(("sec", "lon"))
    block_count = blocks.shape[0]
    cell_count = blocks.shape[1]
    capacity = max(2, 2 * block_count // senders)
    dest_tiles = route_tile[:, :, 0]
    peer_ids = jnp.arange(senders, dtype=jnp.int32)
    slot_ids = jnp.arange(capacity, dtype=jnp.int32).astype(F32)
    own_tiles = lax.dynamic_index_in_dim(dest_tiles, own_index, 0, keepdims=False)
    dest_hot = (own_tiles[:, None] == peer_ids[None, :]).astype(F32)
    order_rank = exclusive_rank(dest_hot, 0)
    slot_index = jnp.sum(order_rank * dest_hot, axis=1)
    slot_hot = (slot_index[:, None] == slot_ids[None, :]).astype(F32)
    selector = (dest_hot[:, :, None] * slot_hot[:, None, :]).reshape(
        block_count, senders * capacity
    )
    outgoing = jnp.dot(selector.T, blocks, precision=lax.Precision.HIGHEST).reshape(
        senders, capacity, cell_count
    )
    incoming = lax.all_to_all(outgoing, ("sec", "lon"), split_axis=0, concat_axis=0, tiled=True)
    arrived = (dest_tiles == own_index).astype(F32)
    arrival_rank = exclusive_rank(arrived, 1)
    slot_take = arrived[:, :, None] * (arrival_rank[:, :, None] == slot_ids[None, None, :]).astype(
        F32
    )
    block_hot = (
        route_block[:, :, None] == jnp.arange(atm_rows, dtype=jnp.int32)[None, None, :]
    ).astype(F32)
    placing = jnp.einsum("syc,sya->asc", slot_take, block_hot, precision=lax.Precision.HIGHEST)
    placing = placing.reshape(atm_rows, senders * capacity)
    return jnp.dot(
        placing, incoming.reshape(senders * capacity, cell_count), precision=lax.Precision.HIGHEST
    )


def per_device(
    shape,
    adjoint_end,
    east_flow,
    east_diff,
    north_flow,
    north_diff,
    vert_diff,
    ocean_mask,
    reaction,
    solubility,
    route_tile,
    route_block,
    xgrid_weights,
    deposition,
):
    adjoint_start, flux = run_ocean(
        shape,
        (
            adjoint_end,
            east_flow,
            east_diff,
            north_flow,
            north_diff,
            vert_diff,
            ocean_mask,
            solubility,
        ),
        reaction,
    )
    blocks = jnp.einsum(
        "bo,boa->ba", flux.astype(jnp.bfloat16), xgrid_weights, preferred_element_type=F32
    )
    flux_adjoint = deliver(blocks, route_tile, route_block, deposition.shape[1])
    ash_adjoint = deposition.astype(F32) * flux_adjoint[None]
    return (adjoint_start, flux_adjoint, ash_adjoint)


def solution(mesh):
    shape = (mesh.shape["sec"], mesh.shape["lat"], mesh.shape["lon"])
    field = P(None, "lat", ("sec", "lon"))
    in_specs = (
        P(None, None, "lat", ("sec", "lon")),
        field,
        field,
        field,
        field,
        field,
        P("lat", ("sec", "lon")),
        P(),
        field,
        P(None, "lat", None),
        P(None, "lat"),
        P("lat", ("sec", "lon"), None),
        field,
    )
    out_specs = (
        P(None, None, "lat", ("sec", "lon")),
        P("lat", ("sec", "lon")),
        field,
    )
    return jax.shard_map(
        functools.partial(per_device, shape),
        mesh=mesh,
        in_specs=in_specs,
        out_specs=out_specs,
        check_vma=False,
    )
```
